256 devices in a mesh: grp: 8 (over x_hi, y), tp: 32 (over x_lo, z, core).
Axes of the slice: x: 4 (x_hi: 2, x_lo: 2; x = x_hi * 2 + x_lo), y: 4, z: 8, core: 2. Of those that a mesh axis runs over, the one named last changes fastest.
Arguments:
- tokens: bfloat16 [49152, 8192], P(('grp', 'tp')), may hold values from -30 to 30
- grad_up: bfloat16 [49152, 14336], P(('grp', 'tp')), may hold values from -24 to 24
- factor_down: float32 [32, 8192], P(None, 'grp'), may hold values from -6 to 6
- factor_up: float32 [14336, 32], P('tp'), may hold values from -18 to 18
- base_weight: bfloat16 [8192, 14336], P('grp', 'tp'), may hold values from -6 to 6
Outputs:
- new_down: float32 [32, 8192], P(None, 'grp')
- new_up: float32 [14336, 32], P('tp')
- merged: bfloat16 [8192, 14336], P('grp', 'tp')
The draws below stay inside these ranges and needn't reach their ends.
All inputs are finite; a program needn't handle non-finite values.
Results may differ from the reference program's by a relative error of at most 0.0046.
The reference program's roundings to bfloat16 on the way (of `reduced` and `returned`) count: a program that leaves them out, or rounds other values in their place, can miss the bound.
Values may be sent and summed in bfloat16 or wider, within the bound.
No kernel may reach another device: no remote copies, remote signals or barrier semaphores. Data moves between devices by JAX's collectives and lax.ppermute only.
A program may use at most 64 MiB of HBM per device.

```python
import jax
import jax.numpy as jnp
from jax import lax

D = 8192
F = 14336
R = 32
TOK_DEV = 192
TOKENS = 49152


def draw_tokens(key, part):
    key = jax.random.fold_in(key, 11)
    position = jnp.arange(D, dtype=jnp.float32) / D
    values = jnp.clip(jax.random.normal(key, (TOKENS, D), jnp.float32), -6.0, 6.0)
    scale = 0.5 * jnp.power(10.0, position)
    return (values * scale[None, :]).astype(jnp.bfloat16)


def draw_factor_up(key, part):
    key = jax.random.fold_in(key, 23)
    position = jnp.arange(F, dtype=jnp.float32) / F
    values = jnp.clip(jax.random.normal(key, (F, R), jnp.float32), -6.0, 6.0)
    scale = 0.3 * jnp.power(10.0, position)
    return (values * scale[:, None]).astype(jnp.float32)


def strengthened(values, key, source, target, shards_of, factor):
    owner, partner = [(jnp.arange(values.shape[axis_at]) // (values.shape[axis_at] // shards_of)).reshape([-1 if axis == axis_at else 1 for axis in range(values.ndim)]) for axis_at in (source, target)]
    chosen = jax.random.permutation(key, shards_of)[partner]
    strong = (owner == chosen) | (owner == (partner + shards_of // 2) % shards_of)
    return jnp.where(strong, factor * values, values)


def shard_levels(own_key, dims, split, smallest, top_value):
    def one(axis_at, shards_of):
        draws = jax.random.uniform(jax.random.fold_in(jax.random.fold_in(own_key, 6), axis_at), (shards_of,), jnp.float32, smallest / len(split), top_value / len(split))
        return jnp.repeat(jnp.exp(draws), dims[axis_at] // shards_of).reshape((-1,) + (1,) * (len(dims) - axis_at - 1))

    factor_of = one(*split[0])
    for cut in split[1:]:
        factor_of = factor_of * one(*cut)
    return factor_of


def scatter_about(key, shape, spread, reach, pieces=(), kind=jnp.bfloat16):
    entries = jax.random.normal(key, shape, jnp.float32) * spread
    if len(pieces) > 0:
        entries = shard_levels(key, shape, pieces, -0.22, 0.18) * entries
    return jnp.clip(entries, min=-reach, max=reach).astype(kind)


def noise_with(key, extent, width, reach, cuts, heavy, held_as=jnp.bfloat16):
    array = width * jax.random.normal(key, extent, jnp.float32)
    if cuts:
        array = array * shard_levels(key, extent, cuts, -0.22, 0.18)
    return jnp.clip(strengthened(array, jax.random.fold_in(key, 3), *heavy), -reach, reach).astype(held_as)


def setup_inputs(seed: int = 0) -> dict:
    arg_keys = jax.random.split(jax.random.key(seed), 6)
    return {
        "tokens": draw_tokens(jax.random.fold_in(arg_keys[5], 71), 0),
        "grad_up": noise_with(arg_keys[1], (TOKENS, F), 1.0, 24.0, ((0, 256),), (0, 1, 256, 6.0)),
        "factor_down": scatter_about(arg_keys[2], (R, D), 1.0, 6.0, ((1, 8),), jnp.float32),
        "factor_up": draw_factor_up(jax.random.fold_in(arg_keys[5], 71), 0),
        "base_weight": scatter_about(arg_keys[4], (D, F), 1.0, 6.0, ((0, 8), (1, 32))),
    }


adapter_scale = 0.25
step_size = 0.1
norm_eps = 1e-06

def reference(tokens, grad_up, factor_down, factor_up, base_weight):
    down_half = factor_down.astype(jnp.bfloat16)
    up_half = factor_up.astype(jnp.bfloat16)
    reduced = jnp.dot(tokens, down_half.T, preferred_element_type=jnp.float32).astype(jnp.bfloat16)
    returned = jnp.dot(grad_up, up_half, preferred_element_type=jnp.float32).astype(jnp.bfloat16)

    def accumulate(block_index, sums_pair):
        offset = block_index.astype(jnp.int32) * TOK_DEV
        grad_rows = lax.dynamic_slice_in_dim(grad_up, offset, TOK_DEV, 0)
        token_rows = lax.dynamic_slice_in_dim(tokens, offset, TOK_DEV, 0)
        low_rows = lax.dynamic_slice_in_dim(reduced, offset, TOK_DEV, 0)
        back_rows = lax.dynamic_slice_in_dim(returned, offset, TOK_DEV, 0)
        sum_b = sums_pair[0] + jnp.dot(grad_rows.T, low_rows, preferred_element_type=jnp.float32)
        sum_a = sums_pair[1] + jnp.dot(back_rows.T, token_rows, preferred_element_type=jnp.float32)
        return (sum_b, sum_a)
    start_pair = (jnp.zeros((F, R), jnp.float32), jnp.zeros((R, D), jnp.float32))
    sum_b, sum_a = lax.fori_loop(0, TOKENS // TOK_DEV, accumulate, start_pair)
    grad_b = adapter_scale * sum_b
    grad_a = adapter_scale * sum_a
    norm_a = jnp.sqrt(jnp.sum(factor_down * factor_down))
    norm_b = jnp.sqrt(jnp.sum(factor_up * factor_up))
    gnorm_a = jnp.sqrt(jnp.sum(grad_a * grad_a) + norm_eps)
    gnorm_b = jnp.sqrt(jnp.sum(grad_b * grad_b) + norm_eps)
    new_down = factor_down - step_size * (norm_a / gnorm_a) * grad_a
    new_up = factor_up - step_size * (norm_b / gnorm_b) * grad_b
    product = jnp.dot(new_down.astype(jnp.bfloat16).T, new_up.astype(jnp.bfloat16).T, preferred_element_type=jnp.float32)
    merged = (base_weight.astype(jnp.float32) + adapter_scale * product).astype(jnp.bfloat16)
    return (new_down, new_up, merged)
```

```python
import jax
import jax.numpy as jnp
from jax import lax
from jax.sharding import Mesh, PartitionSpec as P

adapter_scale = 0.25
step_size = 0.1
norm_eps = 1e-06

GRP = ("xh", "y")
TP = ("xl", "z", "c")
PLANE = ("xh", "y", "xl")
COLUMN = ("z", "c")


def spread(block, axes, count):
    return lax.all_to_all(
        jnp.broadcast_to(block[None], (count,) + block.shape), axes, 0, 0, tiled=True
    )


def shards(tokens, grad_up, factor_down, factor_up, base_weight):
    f32, bf16 = jnp.float32, jnp.bfloat16
    group = lax.axis_index(GRP)
    half = lax.axis_index("xl")
    core = lax.axis_index("c")

    down_half = lax.dynamic_slice_in_dim(factor_down.astype(bf16), core * 16, 16, 0)
    up_t = factor_up.T.astype(bf16)
    downs = spread(down_half, GRP, 8)
    ups = spread(up_t, ("xl", "z"), 16)
    downs = lax.all_gather(downs, "c", axis=0)
    ups = lax.all_gather(ups, "c", axis=1)
    down = downs.transpose(0, 2, 1, 3).reshape(32, 8192)
    up = ups.reshape(32, 32, 448).transpose(1, 0, 2).reshape(32, 14336)

    contract_last = (((1,), (1,)), ((), ()))
    contract_first = (((0,), (0,)), ((), ()))
    reduced = lax.dot_general(tokens, down, contract_last, preferred_element_type=f32).astype(bf16)
    returned = lax.dot_general(grad_up, up, contract_last, preferred_element_type=f32).astype(bf16)
    part_a = lax.dot_general(returned, tokens, contract_first, preferred_element_type=f32)
    part_b = lax.dot_general(reduced, grad_up, contract_first, preferred_element_type=f32)

    part_a = part_a.astype(bf16).reshape(2, 16, 8, 1024)
    part_b = part_b.astype(bf16).reshape(2, 16, 8, 1792)
    part = jnp.concatenate([part_a, part_b], 3).transpose(2, 0, 1, 3).reshape(16, 16, 2816)
    part = lax.all_to_all(part, PLANE, 0, 0, tiled=True)
    part = jnp.sum(part.astype(f32), axis=0).astype(bf16)
    part = lax.all_to_all(part.reshape(16, 22, 128), COLUMN, 0, 0, tiled=True)
    row = adapter_scale * jnp.sum(part.astype(f32), axis=0)
    squares = row * row
    sums = jnp.stack(
        [
            jnp.sum(squares[:8]),
            jnp.sum(squares[8:]),
            jnp.sum(factor_down * factor_down) * (1 / 32),
            jnp.sum(factor_up * factor_up) * (1 / 8),
        ]
    )

    row = jnp.concatenate([row, jnp.broadcast_to(sums[:, None], (4, 128)).reshape(4, 128)], 0)
    rows = spread(row, PLANE, 16).reshape(8, 2, 26, 128)
    sums = jnp.sum(rows[:, :, 22:], axis=(0, 1))
    row_a = lax.dynamic_index_in_dim(rows, group, 0, keepdims=False)[:, :8].reshape(2, 1024)
    row_b = lax.dynamic_slice_in_dim(rows[:, :, 8:22], half * 4, 4, 0)
    row_b = row_b.reshape(4, 2, 4, 448).transpose(0, 2, 1, 3).reshape(16, 2, 448)
    send = jnp.concatenate(
        [
            jnp.broadcast_to(row_a[None], (16, 2, 1024)),
            row_b,
            jnp.broadcast_to(sums[:, :16].reshape(1, 1, 64), (16, 2, 64)),
        ],
        2,
    )
    got = lax.all_to_all(send.reshape(16, 24, 128), COLUMN, 0, 0, tiled=True)
    got = got.reshape(16, 2, 1536).transpose(1, 0, 2).reshape(32, 1536)
    grad_a = got[:, :1024]
    grad_b = got[:, 1024:1472]
    sums = jnp.sum(got[:16, 1472:], axis=0).reshape(4, 16)[:, 0]

    ratio_a = jnp.sqrt(sums[2]) / jnp.sqrt(sums[0] + norm_eps)
    ratio_b = jnp.sqrt(sums[3]) / jnp.sqrt(sums[1] + norm_eps)
    new_down = factor_down - step_size * ratio_a * grad_a
    new_up = factor_up.T - step_size * ratio_b * grad_b
    product = lax.dot_general(
        new_down.astype(bf16), new_up.astype(bf16), contract_first, preferred_element_type=f32
    )
    merged = (base_weight.astype(f32) + adapter_scale * product).astype(bf16)
    return (new_down, new_up.T, merged)


def solution(mesh):
    fine = Mesh(mesh.devices.reshape(2, 4, 2, 8, 2), ("xh", "y", "xl", "z", "c"))
    return jax.shard_map(
        shards,
        mesh=fine,
        in_specs=(
            P(GRP + TP, None),
            P(GRP + TP, None),
            P(None, GRP),
            P(TP, None),
            P(GRP, TP),
        ),
        out_specs=(P(None, GRP), P(TP, None), P(GRP, TP)),
        check_vma=False,
    )
```

```python
import jax
import jax.numpy as jnp
from jax import lax
from jax.experimental import pallas as pl
from jax.experimental.pallas import tpu as pltpu
from jax.sharding import Mesh, PartitionSpec as P

adapter_scale = 0.25
step_size = 0.1
norm_eps = 1e-06

GRP = ("xh", "y")
TP = ("xl", "z", "c")
PLANE = ("xh", "y", "xl")
COLUMN = ("z", "c")
f32, bf16 = jnp.float32, jnp.bfloat16
ALONG_LANES = (((1,), (1,)), ((), ()))
VMEM = pl.BlockSpec(memory_space=pltpu.VMEM)
SMEM = pl.BlockSpec(memory_space=pltpu.SMEM)
HBM = pl.BlockSpec(memory_space=pltpu.HBM)


def in_vmem(x):
    return pltpu.with_memory_space_constraint(x, pltpu.VMEM)


def in_hbm(x):
    return pltpu.with_memory_space_constraint(x, pltpu.HBM)


def exchange(x, axes):
    return lax.all_to_all(x, axes, 0, 0, tiled=True)


def load_kernel(tokens_hbm, grads_hbm, factor_down, factor_up, tokens, grads, norms, sems):
    copies = []
    for n, (source, target) in enumerate(((tokens_hbm, tokens), (grads_hbm, grads))):
        for k in range(4):
            rows = pl.ds(48 * k, 48)
            copies.append(pltpu.make_async_copy(source.at[rows], target.at[rows], sems.at[4 * n + k]))
    for copy in copies:
        copy.start()
    down, up = factor_down[...], factor_up[...]
    norms[...] = jnp.zeros((8, 128), f32)
    norms[0:1] = jnp.full((1, 128), jnp.sum(down * down) * (1 / 4096), f32)
    norms[1:2] = jnp.full((1, 128), jnp.sum(up * up) * (1 / 1024), f32)
    for copy in copies:
        copy.wait()


def gradients_kernel(
    place, tokens, grads, down0, down1, down2, down3, ups, ups_other, out
):
    owned = []
    for ky, blocks in enumerate((down0, down1, down2, down3)):
        for kx in range(2):
            owner = (place[0] ^ kx) * 4 + (place[1] ^ ky)
            columns = pl.ds(pl.multiple_of(owner * 1024, 1024), 1024)
            owned.append((columns, blocks, kx))
    reduced = jnp.zeros((192, 32), f32)
    for n, (columns, blocks, kx) in enumerate(owned):
        reduced += lax.dot_general(
            tokens[:, columns], blocks[kx], ALONG_LANES, preferred_element_type=f32
        )
    reduced_t = reduced.T.astype(bf16)
    returned = jnp.zeros((192, 32), f32)
    for pair in range(16):
        for other, blocks in enumerate((ups, ups_other)):
            start = pair * 896 + (place[3] ^ other) * 384
            columns = pl.ds(pl.multiple_of(start, 128), 512)
            returned += lax.dot_general(
                grads[:, columns], blocks[pair], ALONG_LANES, preferred_element_type=f32
            )
    returned_t = returned.T.astype(bf16)
    for g in range(8):
        part_b = jnp.dot(reduced_t, grads[:, g * 1792 : (g + 1) * 1792], preferred_element_type=f32)
        part_a = jnp.dot(returned_t, tokens[:, g * 1024 : (g + 1) * 1024], preferred_element_type=f32)
        for h in range(2):
            out[2 * g + h, :, :1024] = part_a[16 * h : 16 * h + 16].astype(bf16)
            out[2 * g + h, :, 1024:] = part_b[16 * h : 16 * h + 16].astype(bf16)


def plane_sum_kernel(parts, out, rows):
    for j in range(22):
        columns = slice(128 * j, 128 * j + 128)
        total = parts[0, :, columns].astype(f32)
        for k in range(1, 16):
            total += parts[k, :, columns].astype(f32)
        for h in range(2):
            rows[pl.ds(8 * h * 25 + j, 8, 25), :] = total[8 * h : 8 * h + 8]
    for r in range(16):
        out[r] = rows[pl.ds(r * 25, 22), :].astype(bf16)


def column_sum_kernel(norms, parts, out, rows):
    total = parts[0].astype(f32)
    for k in range(1, 16):
        total += parts[k].astype(f32)
    total = adapter_scale * total
    squares = total * total
    rows[...] = jnp.zeros((32, 128), f32)
    rows[pl.ds(0, 22), :] = total
    sums = (
        jnp.sum(squares[:8], axis=0, keepdims=True),
        jnp.sum(squares[8:], axis=0, keepdims=True),
        norms[0:1],
        norms[1:2],
    )
    for k, line in enumerate(sums):
        high = line.astype(bf16).astype(f32)
        rows[pl.ds(24 + k, 1), :] = high
        rows[pl.ds(28 + k, 1), :] = line - high
    block = rows[...].astype(bf16)
    for k in range(16):
        out[k] = block


def reroute_kernel(place, parts, out, rows):
    group, half = place[0] * 4 + place[1], place[2]
    sums = jnp.zeros((4, 128), f32)
    for g in range(8):
        for h in range(2):
            block = parts[2 * g + h].astype(f32)
            sums += block[24:28] + block[28:32]
    high = sums.astype(bf16).astype(f32)
    low = sums - high
    for h in range(2):
        mine = parts[2 * group + h].astype(f32)[:8]
        for section in range(4):
            block = parts[2 * (half * 4 + section) + h].astype(f32)
            for odd in range(2):
                for core in range(2):
                    start = 8 + 7 * odd + 3 * core
                    rows[(2 * section + odd) * 2 + core, pl.ds(16 * h, 8), :] = mine
                    rows[(2 * section + odd) * 2 + core, pl.ds(16 * h + 8, 4), :] = block[start : start + 4]
                    rows[(2 * section + odd) * 2 + core, pl.ds(16 * h + 12, 4), :] = low if h else high
    for k in range(16):
        out[k] = rows[k].astype(bf16)


def update_kernel(place, parts, factor_down, factor_up, base, new_down, new_up, merged, rows):
    sums = jnp.zeros((4, 128), f32)
    for k in range(16):
        block = parts[k].astype(f32)
        rows[pl.ds(k * 33, 32), :] = block
        sums += block[12:16] + block[28:32]
    sums = jnp.sum(sums, axis=1, keepdims=True)
    scale_a = step_size * jnp.sqrt(sums[2:3]) / jnp.sqrt(sums[0:1] + norm_eps)
    scale_b = step_size * jnp.sqrt(sums[3:4]) / jnp.sqrt(sums[1:2] + norm_eps)

    def ranks(j):
        tiles = [rows[pl.ds(8 * q * 33 + 16 * h + j, 8, 33), :] for h in range(2) for q in range(2)]
        return jnp.concatenate(tiles, 0)

    for j in range(8):
        columns = slice(128 * j, 128 * j + 128)
        new_down[:, columns] = factor_down[:, columns] - scale_a * ranks(j)
    grad_b = jnp.concatenate([ranks(8 + j) for j in range(4)], 1)
    grad_b = jnp.where(place[3] == 0, grad_b, pltpu.roll(grad_b, 448, 1))[:, :448]
    new_up[...] = factor_up[...] - scale_b * grad_b
    left = new_up[...].T.astype(bf16)
    right = new_down[...].astype(bf16)
    for k in range(7):
        lines = slice(64 * k, 64 * k + 64)
        product = jnp.dot(left[lines], right, preferred_element_type=f32)
        merged[lines] = (base[lines].astype(f32) + adapter_scale * product).astype(bf16)


def shards(tokens, grad_up, factor_down, factor_up, base_weight):
    place = jnp.stack([lax.axis_index(name) for name in ("xh", "y", "xl", "c")]).astype(jnp.int32)
    factor_up = factor_up.T

    up = factor_up.astype(bf16)
    up = jnp.where(place[3] == 0, jnp.pad(up, ((0, 0), (0, 64))), jnp.pad(up, ((0, 0), (64, 0))))
    ups = exchange(jnp.broadcast_to(up[None], (16, 32, 512)), ("xl", "z"))
    down = factor_down.astype(bf16)
    down0 = jnp.stack([down, lax.ppermute(down, "xh", [(0, 1), (1, 0)])])
    downs = [down0] + [lax.ppermute(down0, "y", [(i, i ^ k) for i in range(4)]) for k in (1, 2, 3)]
    ups, downs = lax.optimization_barrier((ups, downs))
    ups_other = lax.ppermute(ups, "c", [(0, 1), (1, 0)])
    tokens, grad_up, norms = pl.pallas_call(
        load_kernel,
        out_shape=(
            pltpu.VMEM((192, 8192), bf16),
            pltpu.VMEM((192, 14336), bf16),
            jax.ShapeDtypeStruct((8, 128), f32),
        ),
        in_specs=[HBM, HBM, VMEM, VMEM],
        out_specs=(VMEM, VMEM, VMEM),
        scratch_shapes=[pltpu.SemaphoreType.DMA((8,))],
        compiler_params=pltpu.CompilerParams(vmem_limit_bytes=16 * 1024 * 1024),
        cost_estimate=pl.CostEstimate(flops=0, bytes_accessed=17 * 1024 * 1024, transcendentals=0),
        name="load",
    )(in_hbm(tokens), in_hbm(grad_up), factor_down, factor_up)
    params = pltpu.CompilerParams(vmem_limit_bytes=24 * 1024 * 1024)
    parts = pl.pallas_call(
        gradients_kernel,
        out_shape=jax.ShapeDtypeStruct((16, 16, 2816), bf16),
        in_specs=[SMEM] + [VMEM] * 8,
        out_specs=VMEM,
        compiler_params=params,
        name="gradients",
    )(place, tokens, grad_up, *downs, ups, ups_other)
    parts = in_vmem(exchange(parts, PLANE))
    parts = pl.pallas_call(
        plane_sum_kernel,
        out_shape=jax.ShapeDtypeStruct((16, 22, 128), bf16),
        in_specs=[VMEM],
        out_specs=VMEM,
        scratch_shapes=[pltpu.VMEM((400, 128), f32)],
        name="plane_sum",
    )(parts)
    parts = in_vmem(exchange(parts, COLUMN))
    parts = pl.pallas_call(
        column_sum_kernel,
        out_shape=jax.ShapeDtypeStruct((16, 32, 128), bf16),
        in_specs=[VMEM, VMEM],
        out_specs=VMEM,
        scratch_shapes=[pltpu.VMEM((32, 128), f32)],
        name="column_sum",
    )(norms, parts)
    parts = in_vmem(exchange(parts, PLANE))
    parts = pl.pallas_call(
        reroute_kernel,
        out_shape=jax.ShapeDtypeStruct((16, 32, 128), bf16),
        in_specs=[SMEM, VMEM],
        out_specs=VMEM,
        scratch_shapes=[pltpu.VMEM((16, 32, 128), f32)],
        name="reroute",
    )(place, parts)
    parts = in_vmem(exchange(parts, COLUMN))
    new_down, new_up, merged = pl.pallas_call(
        update_kernel,
        out_shape=(
            jax.ShapeDtypeStruct((32, 1024), f32),
            jax.ShapeDtypeStruct((32, 448), f32),
            jax.ShapeDtypeStruct((448, 1024), bf16),
        ),
        in_specs=[SMEM] + [VMEM] * 4,
        out_specs=(VMEM, VMEM, VMEM),
        scratch_shapes=[pltpu.VMEM((528, 128), f32)],
        name="update",
    )(place, parts, factor_down, factor_up, base_weight.T)
    return (new_down, new_up.T, merged.T)


def solution(mesh):
    fine = Mesh(mesh.devices.reshape(2, 4, 2, 8, 2), ("xh", "y", "xl", "z", "c"))
    return jax.shard_map(
        shards,
        mesh=fine,
        in_specs=(
            P(GRP + TP, None),
            P(GRP + TP, None),
            P(None, GRP),
            P(TP, None),
            P(GRP, TP),
        ),
        out_specs=(P(None, GRP), P(TP, None), P(GRP, TP)),
        check_vma=False,
    )
```

```python
import jax
import jax.numpy as jnp
from jax import lax
from jax.experimental import pallas as pl
from jax.experimental.pallas import tpu as pltpu
from jax.sharding import Mesh, PartitionSpec as P

adapter_scale = 0.25
step_size = 0.1
norm_eps = 1e-06

GRP = ("xh", "y")
TP = ("xl", "z", "c")
PLANE = ("xh", "y", "xl")
COLUMN = ("z", "c")
f32, bf16 = jnp.float32, jnp.bfloat16
ALONG_LANES = (((1,), (1,)), ((), ()))
VMEM = pl.BlockSpec(memory_space=pltpu.VMEM)
SMEM = pl.BlockSpec(memory_space=pltpu.SMEM)
HBM = pl.BlockSpec(memory_space=pltpu.HBM)


def exchange(x, axes):
    return lax.all_to_all(x, axes, 0, 0, tiled=True)


def prepare_kernel(down_hbm, up_hbm, down, ups, factor_down, factor_up, sems):
    copies = [
        pltpu.make_async_copy(down_hbm, factor_down, sems.at[0]),
        pltpu.make_async_copy(up_hbm, factor_up, sems.at[1]),
    ]
    for copy in copies:
        copy.start()
    for copy in copies:
        copy.wait()
    down[...] = factor_down[...].astype(bf16)
    up = jnp.concatenate([factor_up[...], jnp.zeros((32, 64), f32)], 1)
    up = jnp.where(lax.axis_index("c") == 0, up, pltpu.roll(up, 64, 1)).astype(bf16)
    for k in range(16):
        ups[k] = up


def own_ranks_first(low, core):
    low = low.T
    return jnp.where(core == 0, low, jnp.concatenate([low[16:], low[:16]], 0)).astype(bf16)


def grad_b_kernel(
    place, tokens_hbm, grads_hbm, down0, down1, down2, down3, keep, give, tokens, grads, down, sems
):
    copies = []
    for n, (source, target) in enumerate(((tokens_hbm, tokens), (grads_hbm, grads))):
        width = source.shape[1] // 8
        for k in range(8):
            columns = pl.ds(width * k, width)
            copies.append(
                pltpu.make_async_copy(source.at[:, columns], target.at[:, columns], sems.at[8 * n + k])
            )
    for copy in copies:
        copy.start()
    for ky, blocks in enumerate((down0, down1, down2, down3)):
        for kx in range(2):
            owner = (place[0] ^ kx) * 4 + (place[1] ^ ky)
            down[:, pl.ds(pl.multiple_of(owner * 1024, 1024), 1024)] = blocks[kx]
    reduced = jnp.zeros((192, 32), f32)
    for q in range(4):
        columns = slice(2048 * q, 2048 * q + 2048)
        copies[2 * q].wait()
        copies[2 * q + 1].wait()
        reduced += lax.dot_general(
            tokens[:, columns], down[:, columns], ALONG_LANES, preferred_element_type=f32
        )
    left = own_ranks_first(reduced, place[3])
    for p in range(16):
        if p % 2 == 0:
            copies[8 + p // 2].wait()
        part = jnp.dot(left, grads[:, p * 896 : (p + 1) * 896], preferred_element_type=f32)
        keep[p] = part[:16].astype(bf16)
        give[p] = part[16:].astype(bf16)


def grad_a_kernel(place, tokens, grads, ups, ups_other, keep, give, up):
    for pair in range(16):
        mine, other = ups[pair], ups_other[pair]
        first = jnp.where(place[3] == 0, mine, other)
        second = jnp.where(place[3] == 0, other, mine)
        start = pair * 896
        up[:, start : start + 384] = first[:, :384]
        up[:, start + 384 : start + 512] = first[:, 384:] + second[:, :128]
        up[:, start + 512 : start + 896] = second[:, 128:]
    returned = lax.dot_general(grads[...], up[...], ALONG_LANES, preferred_element_type=f32)
    left = own_ranks_first(returned, place[3])
    for p in range(16):
        part = jnp.dot(left, tokens[:, p * 512 : (p + 1) * 512], preferred_element_type=f32)
        keep[p] = part[:16].astype(bf16)
        give[p] = part[16:].astype(bf16)


def chip_sum_kernel(keep_a, got_a, keep_b, got_b, out):
    for p in range(16):
        out[p, :, :512] = (keep_a[p].astype(f32) + got_a[p].astype(f32)).astype(bf16)
        out[p, :, 512:] = (keep_b[p].astype(f32) + got_b[p].astype(f32)).astype(bf16)


def plane_sum_kernel(parts, out, rows):
    for j in range(11):
        columns = slice(128 * j, 128 * j + 128)
        total = parts[0, :, columns].astype(f32)
        for k in range(1, 16):
            total += parts[k, :, columns].astype(f32)
        for i in range(2):
            rows[pl.ds(11 * i + j, 8, 23), :] = total[8 * i : 8 * i + 8]
    for z in range(8):
        out[z] = rows[pl.ds(23 * z, 22), :].astype(bf16)


def z_sum_kernel(parts, factor_down, factor_up, out, rows):
    total = parts[0].astype(f32)
    for k in range(1, 8):
        total += parts[k].astype(f32)
    total = adapter_scale * total
    squares = total * total

    def squared(*pieces):
        return sum(jnp.sum(squares[a:b], axis=0, keepdims=True) for a, b in pieces)

    down, up = factor_down[...], factor_up[...]
    rows[...] = jnp.zeros((32, 128), f32)
    rows[pl.ds(0, 22), :] = total
    sums = (
        squared((0, 4), (11, 15)),
        squared((4, 11), (15, 22)),
        jnp.full((1, 128), jnp.sum(down * down) * (1 / 4096), f32),
        jnp.full((1, 128), jnp.sum(up * up) * (1 / 1024), f32),
    )
    for k, line in enumerate(sums):
        high = line.astype(bf16).astype(f32)
        rows[pl.ds(24 + k, 1), :] = high
        rows[pl.ds(28 + k, 1), :] = line - high
    block = rows[...].astype(bf16)
    for k in range(16):
        out[k] = block


def reroute_kernel(place, parts, out, rows):
    group, half = place[0] * 4 + place[1], place[2]
    sums = jnp.zeros((4, 128), f32)
    for p in range(16):
        block = parts[p].astype(f32)
        sums += block[24:28] + block[28:32]
    high = sums.astype(bf16).astype(f32)
    low = sums - high
    mine = [parts[2 * group + k].astype(f32) for k in range(2)]
    for z in range(8):
        block = parts[8 * half + z].astype(f32)
        for core in range(2):
            k = 2 * z + core
            for i in range(2):
                rows[k, pl.ds(16 * i, 4), :] = mine[0][11 * i : 11 * i + 4]
                rows[k, pl.ds(16 * i + 4, 4), :] = mine[1][11 * i : 11 * i + 4]
                start = 11 * i + 4 + 3 * core
                rows[k, pl.ds(16 * i + 8, 4), :] = block[start : start + 4]
                rows[k, pl.ds(16 * i + 12, 4), :] = low if i else high
            out[k] = rows[k].astype(bf16)


def update_kernel(place, parts, factor_down, factor_up, base, new_down, new_up, merged, rows):
    sums = jnp.zeros((4, 128), f32)
    for k in range(16):
        block = parts[k].astype(f32)
        rows[pl.ds(k * 33, 32), :] = block
        sums += block[12:16] + block[28:32]
    sums = jnp.sum(sums, axis=1, keepdims=True)
    scale_a = step_size * jnp.sqrt(sums[2:3]) / jnp.sqrt(sums[0:1] + norm_eps)
    scale_b = step_size * jnp.sqrt(sums[3:4]) / jnp.sqrt(sums[1:2] + norm_eps)

    def ranks(j):
        tiles = [rows[pl.ds(33 * core + 16 * i + j, 8, 66), :] for core in range(2) for i in range(2)]
        return jnp.concatenate(tiles, 0)

    for j in range(8):
        columns = slice(128 * j, 128 * j + 128)
        new_down[:, columns] = factor_down[:, columns] - scale_a * ranks(j)
    grad_b = jnp.concatenate([ranks(8 + j) for j in range(4)], 1)
    grad_b = jnp.where(place[3] == 0, grad_b, pltpu.roll(grad_b, 448, 1))[:, :448]
    new_up[...] = factor_up[...] - scale_b * grad_b
    left = new_up[...].T.astype(bf16)
    right = new_down[...].astype(bf16)
    for k in range(7):
        lines = slice(64 * k, 64 * k + 64)
        product = jnp.dot(left[lines], right, preferred_element_type=f32)
        merged[lines] = (base[lines].astype(f32) + adapter_scale * product).astype(bf16)


def kernel(body, outs, args, scratch=(), in_hbm=(), mib=16, flops=0, moved=0):
    specs, placed = [], []
    for n, a in enumerate(args):
        if jnp.issubdtype(a.dtype, jnp.integer):
            specs.append(SMEM)
        else:
            specs.append(HBM if n in in_hbm else VMEM)
            a = pltpu.with_memory_space_constraint(a, pltpu.HBM if n in in_hbm else pltpu.VMEM)
        placed.append(a)
    return pl.pallas_call(
        body,
        out_shape=outs,
        in_specs=specs,
        out_specs=jax.tree.map(lambda _: VMEM, outs),
        scratch_shapes=list(scratch),
        compiler_params=pltpu.CompilerParams(vmem_limit_bytes=mib * 1024 * 1024),
        cost_estimate=pl.CostEstimate(flops=flops, bytes_accessed=moved, transcendentals=0),
        name=body.__name__,
    )(*placed)


def swap(x, axis):
    return lax.ppermute(x, axis, [(0, 1), (1, 0)])


def shards(tokens, grad_up, factor_down, factor_up, base_weight):
    place = jnp.stack([lax.axis_index(name) for name in ("xh", "y", "xl", "c")]).astype(jnp.int32)
    factor_up = factor_up.T
    shape = jax.ShapeDtypeStruct

    down, up = kernel(
        prepare_kernel,
        (shape((32, 1024), bf16), shape((16, 32, 512), bf16)),
        (factor_down, factor_up),
        [pltpu.VMEM((32, 1024), f32), pltpu.VMEM((32, 448), f32), pltpu.SemaphoreType.DMA((2,))],
        in_hbm=(0, 1),
    )
    down_far = swap(down, "xh")
    ups = exchange(up, ("xl", "z"))
    down0 = jnp.stack([down, down_far])
    downs = [down0] + [lax.ppermute(down0, "y", [(i, i ^ k) for i in range(4)]) for k in (1, 2, 3)]
    ups, downs = lax.optimization_barrier((ups, downs))
    ups_other = swap(ups, "c")

    keep_b, give_b, tokens, grad_up = kernel(
        grad_b_kernel,
        [shape((16, 16, 896), bf16)] * 2 + [pltpu.VMEM((192, 8192), bf16), pltpu.VMEM((192, 14336), bf16)],
        [place, tokens, grad_up] + downs,
        [pltpu.VMEM((32, 8192), bf16), pltpu.SemaphoreType.DMA((16,))],
        in_hbm=(1, 2),
        flops=300000000,
        moved=10 * 1024 * 1024,
    )
    got_b = swap(give_b, "c")
    keep_a, give_a = kernel(
        grad_a_kernel,
        [shape((16, 16, 512), bf16)] * 2,
        (place, tokens, grad_up, ups, ups_other),
        [pltpu.VMEM((32, 14336), bf16)],
        flops=300000000,
        moved=10 * 1024 * 1024,
    )
    got_a = swap(give_a, "c")
    args = (keep_a, got_a, keep_b, got_b)
    parts = kernel(chip_sum_kernel, shape((16, 16, 1408), bf16), args)
    parts = exchange(parts, PLANE)
    parts = kernel(plane_sum_kernel, shape((8, 22, 128), bf16), (parts,), [pltpu.VMEM((184, 128), f32)])
    parts = exchange(parts, "z")
    blocks = shape((16, 32, 128), bf16)
    parts = kernel(z_sum_kernel, blocks, (parts, factor_down, factor_up), [pltpu.VMEM((32, 128), f32)])
    parts = exchange(parts, PLANE)
    parts = kernel(reroute_kernel, blocks, (place, parts), [pltpu.VMEM((16, 32, 128), f32)])
    parts = exchange(parts, COLUMN)
    outs = (shape((32, 1024), f32), shape((32, 448), f32), shape((448, 1024), bf16))
    args = (place, parts, factor_down, factor_up, base_weight.T)
    new_down, new_up, merged = kernel(update_kernel, outs, args, [pltpu.VMEM((528, 128), f32)])
    return (new_down, new_up.T, merged.T)


def solution(mesh):
    fine = Mesh(mesh.devices.reshape(2, 4, 2, 8, 2), ("xh", "y", "xl", "z", "c"))
    return jax.shard_map(
        shards,
        mesh=fine,
        in_specs=(
            P(GRP + TP, None),
            P(GRP + TP, None),
            P(None, GRP),
            P(TP, None),
            P(GRP, TP),
        ),
        out_specs=(P(None, GRP), P(TP, None), P(GRP, TP)),
        check_vma=False,
    )
```

```python
import jax
import jax.numpy as jnp
from jax import lax
from jax.experimental import pallas as pl
from jax.experimental.pallas import tpu as pltpu
from jax.sharding import Mesh, PartitionSpec as P

adapter_scale = 0.25
step_size = 0.1
norm_eps = 1e-06

GRP = ("xh", "y")
TP = ("xl", "z", "c")
PLANE = ("xh", "y", "xl")
f32, bf16 = jnp.float32, jnp.bfloat16
ALONG_LANES = (((1,), (1,)), ((), ()))
VMEM = pl.BlockSpec(memory_space=pltpu.VMEM)
SMEM = pl.BlockSpec(memory_space=pltpu.SMEM)
HBM = pl.BlockSpec(memory_space=pltpu.HBM)


def exchange(x, axes):
    return lax.all_to_all(x, axes, 0, 0, tiled=True)


def prepare_kernel(down_hbm, up_hbm, down, ups, factor_down, factor_up, sems):
    copies = [
        pltpu.make_async_copy(down_hbm, factor_down, sems.at[0]),
        pltpu.make_async_copy(up_hbm, factor_up, sems.at[1]),
    ]
    for copy in copies:
        copy.start()
    for copy in copies:
        copy.wait()
    down[...] = factor_down[...].astype(bf16)
    up = jnp.concatenate([factor_up[...], jnp.zeros((32, 64), f32)], 1)
    up = jnp.where(lax.axis_index("c") == 0, up, pltpu.roll(up, 64, 1)).astype(bf16)
    for k in range(16):
        ups[k] = up


def own_ranks_first(low, core):
    low = low.T
    return jnp.where(core == 0, low, jnp.concatenate([low[16:], low[:16]], 0)).astype(bf16)


def grad_b_kernel(
    place, tokens_hbm, grads_hbm, down0, down1, down2, down3, keep, give, tokens, grads, down, sems
):
    copies = []
    for n, (source, target) in enumerate(((tokens_hbm, tokens), (grads_hbm, grads))):
        width = source.shape[1] // 8
        for k in range(8):
            columns = pl.ds(width * k, width)
            copies.append(
                pltpu.make_async_copy(source.at[:, columns], target.at[:, columns], sems.at[8 * n + k])
            )
    for copy in copies:
        copy.start()
    for ky, blocks in enumerate((down0, down1, down2, down3)):
        for kx in range(2):
            owner = (place[0] ^ kx) * 4 + (place[1] ^ ky)
            down[:, pl.ds(pl.multiple_of(owner * 1024, 1024), 1024)] = blocks[kx]
    reduced = jnp.zeros((192, 32), f32)
    for q in range(4):
        columns = slice(2048 * q, 2048 * q + 2048)
        copies[2 * q].wait()
        copies[2 * q + 1].wait()
        reduced += lax.dot_general(
            tokens[:, columns], down[:, columns], ALONG_LANES, preferred_element_type=f32
        )
    left = own_ranks_first(reduced, place[3])
    for p in range(16):
        if p % 2 == 0:
            copies[8 + p // 2].wait()
        part = jnp.dot(left, grads[:, p * 896 : (p + 1) * 896], preferred_element_type=f32)
        keep[:, p * 896 : (p + 1) * 896] = part[:16].astype(bf16)
        give[:, p * 896 : (p + 1) * 896] = part[16:].astype(bf16)


def grad_a_kernel(place, tokens, grads, ups, ups_other, keep, give, up):
    for pair in range(16):
        mine, other = ups[pair], ups_other[pair]
        first = jnp.where(place[3] == 0, mine, other)
        second = jnp.where(place[3] == 0, other, mine)
        start = pair * 896
        up[:, start : start + 384] = first[:, :384]
        up[:, start + 384 : start + 512] = first[:, 384:] + second[:, :128]
        up[:, start + 512 : start + 896] = second[:, 128:]
    returned = lax.dot_general(grads[...], up[...], ALONG_LANES, preferred_element_type=f32)
    left = own_ranks_first(returned, place[3])
    for p in range(16):
        part = jnp.dot(left, tokens[:, p * 512 : (p + 1) * 512], preferred_element_type=f32)
        keep[:, p * 512 : (p + 1) * 512] = part[:16].astype(bf16)
        give[:, p * 512 : (p + 1) * 512] = part[16:].astype(bf16)


def chip_sum_kernel(keep_a, got_a, keep_b, got_b, out, rows):
    tile = 0
    for keep, got in ((keep_a, got_a), (keep_b, got_b)):
        for j in range(keep.shape[1] // 128):
            columns = slice(128 * j, 128 * j + 128)
            total = keep[:, columns].astype(f32) + got[:, columns].astype(f32)
            for h in range(2):
                rows[pl.ds(177 * 8 * h + tile, 8, 177), :] = total[8 * h : 8 * h + 8]
            tile += 1
    for r in range(16):
        out[r] = rows[pl.ds(177 * r, 176), :].astype(bf16)


def plane_sum_kernel(parts, factor_up, out, extra):
    total = parts[0].astype(f32)
    for k in range(1, 16):
        total += parts[k].astype(f32)
    up = factor_up[...]
    line = jnp.full((1, 128), jnp.sum(up * up) * (1 / 8), f32)
    high = line.astype(bf16).astype(f32)
    extra[...] = jnp.zeros((16, 128), f32)
    extra[0:1] = high
    extra[1:2] = line - high
    block, last = total.astype(bf16), extra[...].astype(bf16)
    for k in range(8):
        out[k, :176] = block
        out[k, 176:] = last


def reroute_kernel(parts, factor_down, out, row, rows):
    total = parts[0].astype(f32)
    for k in range(1, 8):
        total += parts[k].astype(f32)
    grads = adapter_scale * total[:176]
    row[...] = grads
    squares = grads * grads
    down = factor_down[...]
    lane = lax.broadcasted_iota(jnp.int32, (1, 128), 1)
    line = jnp.where(
        lane < 64,
        jnp.where(lane < 32, jnp.sum(squares[:64]), jnp.sum(squares[64:])),
        jnp.where(lane < 96, jnp.sum(down * down) * (1 / 4), total[176:177] + total[177:178]),
    )
    high = line.astype(bf16).astype(f32)
    low = line - high
    z = lax.axis_index("z")
    for p in range(16):
        for core in range(2):
            k = 2 * p + core
            rows[k, 0:8] = row[8 * (p // 2) : 8 * (p // 2) + 8]
            rows[k, 8:12] = row[pl.ds(64 + 7 * (8 * (p % 2) + z) + 3 * core, 4), :]
            rows[k, 12:13] = high
            rows[k, 13:14] = low
            rows[k, 14:16] = jnp.zeros((2, 128), f32)
            out[k] = rows[k].astype(bf16)


def update_kernel(place, parts, factor_down, factor_up, base, new_down, new_up, merged, rows):
    line = jnp.zeros((1, 128), f32)
    for k in range(32):
        block = parts[k].astype(f32)
        rows[pl.ds(k * 17, 16), :] = block
        line += block[12:13] + block[13:14]
    scale_a = step_size * jnp.sqrt(line[:, 64:65]) / jnp.sqrt(line[:, 0:1] + norm_eps)
    scale_b = step_size * jnp.sqrt(line[:, 96:97]) / jnp.sqrt(line[:, 32:33] + norm_eps)

    def ranks(j):
        tiles = [rows[pl.ds(17 * core + 272 * h + j, 8, 34), :] for core in range(2) for h in range(2)]
        return jnp.concatenate(tiles, 0)

    for j in range(8):
        columns = slice(128 * j, 128 * j + 128)
        new_down[:, columns] = factor_down[:, columns] - scale_a * ranks(j)
    grad_b = jnp.concatenate([ranks(8 + j) for j in range(4)], 1)
    grad_b = jnp.where(place[3] == 0, grad_b, pltpu.roll(grad_b, 448, 1))[:, :448]
    new_up[...] = factor_up[...] - scale_b * grad_b
    left = new_up[...].T.astype(bf16)
    right = new_down[...].astype(bf16)
    for k in range(7):
        lines = slice(64 * k, 64 * k + 64)
        product = jnp.dot(left[lines], right, preferred_element_type=f32)
        merged[lines] = (base[lines].astype(f32) + adapter_scale * product).astype(bf16)


def kernel(body, outs, args, scratch=(), in_hbm=(), mib=16, flops=0, moved=0):
    specs, placed = [], []
    for n, a in enumerate(args):
        if jnp.issubdtype(a.dtype, jnp.integer):
            specs.append(SMEM)
        else:
            specs.append(HBM if n in in_hbm else VMEM)
            a = pltpu.with_memory_space_constraint(a, pltpu.HBM if n in in_hbm else pltpu.VMEM)
        placed.append(a)
    return pl.pallas_call(
        body,
        out_shape=outs,
        in_specs=specs,
        out_specs=jax.tree.map(lambda _: VMEM, outs),
        scratch_shapes=list(scratch),
        compiler_params=pltpu.CompilerParams(vmem_limit_bytes=mib * 1024 * 1024),
        cost_estimate=pl.CostEstimate(flops=flops, bytes_accessed=moved, transcendentals=0),
        name=body.__name__,
    )(*placed)


def swap(x, axis):
    return lax.ppermute(x, axis, [(0, 1), (1, 0)])


def shards(tokens, grad_up, factor_down, factor_up, base_weight):
    place = jnp.stack([lax.axis_index(name) for name in ("xh", "y", "xl", "c")]).astype(jnp.int32)
    factor_up = factor_up.T
    shape = jax.ShapeDtypeStruct

    down, up = kernel(
        prepare_kernel,
        (shape((32, 1024), bf16), shape((16, 32, 512), bf16)),
        (factor_down, factor_up),
        [pltpu.VMEM((32, 1024), f32), pltpu.VMEM((32, 448), f32), pltpu.SemaphoreType.DMA((2,))],
        in_hbm=(0, 1),
    )
    down_far = swap(down, "xh")
    ups = exchange(up, ("xl", "z"))
    down0 = jnp.stack([down, down_far])
    downs = [down0] + [lax.ppermute(down0, "y", [(i, i ^ k) for i in range(4)]) for k in (1, 2, 3)]
    ups, downs = lax.optimization_barrier((ups, downs))
    ups_other = swap(ups, "c")

    keep_b, give_b, tokens, grad_up = kernel(
        grad_b_kernel,
        [shape((16, 14336), bf16)] * 2 + [pltpu.VMEM((192, 8192), bf16), pltpu.VMEM((192, 14336), bf16)],
        [place, tokens, grad_up] + downs,
        [pltpu.VMEM((32, 8192), bf16), pltpu.SemaphoreType.DMA((16,))],
        in_hbm=(1, 2),
        flops=300000000,
        moved=10 * 1024 * 1024,
    )
    got_b = swap(give_b, "c")
    keep_a, give_a = kernel(
        grad_a_kernel,
        [shape((16, 8192), bf16)] * 2,
        (place, tokens, grad_up, ups, ups_other),
        [pltpu.VMEM((32, 14336), bf16)],
        flops=300000000,
        moved=10 * 1024 * 1024,
    )
    got_a = swap(give_a, "c")
    args = (keep_a, got_a, keep_b, got_b)
    parts = kernel(chip_sum_kernel, shape((16, 176, 128), bf16), args, [pltpu.VMEM((2832, 128), f32)])
    parts = exchange(parts, PLANE)
    parts = kernel(
        plane_sum_kernel, shape((8, 192, 128), bf16), (parts, factor_up), [pltpu.VMEM((16, 128), f32)]
    )
    parts = exchange(parts, "z")
    scratch = [pltpu.VMEM((176, 128), f32), pltpu.VMEM((32, 16, 128), f32)]
    parts = kernel(reroute_kernel, shape((32, 16, 128), bf16), (parts, factor_down), scratch)
    parts = exchange(parts, PLANE + ("c",))
    outs = (shape((32, 1024), f32), shape((32, 448), f32), shape((448, 1024), bf16))
    args = (place, parts, factor_down, factor_up, base_weight.T)
    new_down, new_up, merged = kernel(update_kernel, outs, args, [pltpu.VMEM((544, 128), f32)])
    return (new_down, new_up.T, merged.T)


def solution(mesh):
    fine = Mesh(mesh.devices.reshape(2, 4, 2, 8, 2), ("xh", "y", "xl", "z", "c"))
    return jax.shard_map(
        shards,
        mesh=fine,
        in_specs=(
            P(GRP + TP, None),
            P(GRP + TP, None),
            P(None, GRP),
            P(TP, None),
            P(GRP, TP),
        ),
        out_specs=(P(None, GRP), P(TP, None), P(GRP, TP)),
        check_vma=False,
    )
```

```python
import jax
import jax.numpy as jnp
from jax import lax
from jax.experimental import pallas as pl
from jax.experimental.pallas import tpu as pltpu
from jax.sharding import Mesh, PartitionSpec as P

adapter_scale = 0.25
step_size = 0.1
norm_eps = 1e-06

GRP = ("xh", "y")
TP = ("xl", "zh", "zl", "c")
PLANE = ("xh", "y", "xl")
f32, bf16 = jnp.float32, jnp.bfloat16
ALONG_LANES = (((1,), (1,)), ((), ()))
VMEM = pl.BlockSpec(memory_space=pltpu.VMEM)
SMEM = pl.BlockSpec(memory_space=pltpu.SMEM)
HBM = pl.BlockSpec(memory_space=pltpu.HBM)


def exchange(x, axes):
    return lax.all_to_all(x, axes, 0, 0, tiled=True)


def prepare_kernel(down_hbm, up_hbm, down, ups, factor_down, factor_up, sems):
    copies = [
        pltpu.make_async_copy(down_hbm, factor_down, sems.at[0]),
        pltpu.make_async_copy(up_hbm, factor_up, sems.at[1]),
    ]
    for copy in copies:
        copy.start()
    for copy in copies:
        copy.wait()
    down[...] = factor_down[...].astype(bf16)
    up = jnp.concatenate([factor_up[...], jnp.zeros((32, 64), f32)], 1)
    up = jnp.where(lax.axis_index("c") == 0, up, pltpu.roll(up, 64, 1)).astype(bf16)
    for k in range(16):
        ups[k] = up


def own_ranks_first(low, core):
    low = low.T
    return jnp.where(core == 0, low, jnp.concatenate([low[16:], low[:16]], 0)).astype(bf16)


def grad_b_kernel(
    place, tokens_hbm, grads_hbm, down0, down1, down2, down3, keep, give, tokens, grads, down, sems
):
    copies = []
    for n, (source, target) in enumerate(((tokens_hbm, tokens), (grads_hbm, grads))):
        width = source.shape[1] // 8
        for k in range(8):
            columns = pl.ds(width * k, width)
            copies.append(
                pltpu.make_async_copy(source.at[:, columns], target.at[:, columns], sems.at[8 * n + k])
            )
    for copy in copies:
        copy.start()
    for ky, blocks in enumerate((down0, down1, down2, down3)):
        for kx in range(2):
            owner = (place[0] ^ kx) * 4 + (place[1] ^ ky)
            down[:, pl.ds(pl.multiple_of(owner * 1024, 1024), 1024)] = blocks[kx]
    reduced = jnp.zeros((192, 32), f32)
    for q in range(4):
        columns = slice(2048 * q, 2048 * q + 2048)
        copies[2 * q].wait()
        copies[2 * q + 1].wait()
        reduced += lax.dot_general(
            tokens[:, columns], down[:, columns], ALONG_LANES, preferred_element_type=f32
        )
    left = own_ranks_first(reduced, place[3])
    for p in range(16):
        if p % 2 == 0:
            copies[8 + p // 2].wait()
        part = jnp.dot(left, grads[:, p * 896 : (p + 1) * 896], preferred_element_type=f32)
        keep[:, p * 896 : (p + 1) * 896] = part[:16].astype(bf16)
        give[:, p * 896 : (p + 1) * 896] = part[16:].astype(bf16)


def grad_a_kernel(place, tokens, grads, ups, ups_other, keep, give, up):
    for pair in range(16):
        mine, other = ups[pair], ups_other[pair]
        first = jnp.where(place[3] == 0, mine, other)
        second = jnp.where(place[3] == 0, other, mine)
        start = pair * 896
        up[:, start : start + 384] = first[:, :384]
        up[:, start + 384 : start + 512] = first[:, 384:] + second[:, :128]
        up[:, start + 512 : start + 896] = second[:, 128:]
    returned = lax.dot_general(grads[...], up[...], ALONG_LANES, preferred_element_type=f32)
    left = own_ranks_first(returned, place[3])
    for p in range(16):
        part = jnp.dot(left, tokens[:, p * 512 : (p + 1) * 512], preferred_element_type=f32)
        keep[:, p * 512 : (p + 1) * 512] = part[:16].astype(bf16)
        give[:, p * 512 : (p + 1) * 512] = part[16:].astype(bf16)


def chip_sum_kernel(keep_a, got_a, keep_b, got_b, out, rows):
    tiles = [(keep_a, got_a, 128 * j, j % 8 // 4, j // 8 * 4 + j % 4) for j in range(64)]
    for j in range(112):
        pair, k = divmod(j, 7)
        odd = pair % 2
        half = odd if k < 4 else 1 - odd
        place = 32 + pair // 2 * 7 + (4 - half if odd else 0) + (k if k < 4 else k - 4)
        tiles.append((keep_b, got_b, 128 * j, half, place))
    for keep, got, start, half, place in tiles:
        columns = slice(start, start + 128)
        total = keep[:, columns].astype(f32) + got[:, columns].astype(f32)
        for h in range(2):
            rows[pl.ds(177 * 8 * h + 88 * half + place, 8, 177), :] = total[8 * h : 8 * h + 8]
    for r in range(16):
        for half in range(2):
            out[2 * r + half] = rows[pl.ds(177 * r + 88 * half, 88), :].astype(bf16)


def plane_sum_kernel(parts, factor_up, out, rows):
    total = parts[0].astype(f32)
    for k in range(1, 32):
        total += parts[k].astype(f32)
    up = factor_up[...]
    line = jnp.full((1, 128), jnp.sum(up * up) * (1 / 8), f32)
    high = line.astype(bf16).astype(f32)
    rows[0:88] = total
    rows[88:96] = jnp.zeros((8, 128), f32)
    rows[88:89] = high
    rows[89:90] = line - high
    block = rows[...].astype(bf16)
    for k in range(4):
        out[k] = block


def reroute_kernel(parts, factor_down, out, row, rows):
    total = parts[0].astype(f32)
    for k in range(1, 4):
        total += parts[k].astype(f32)
    grads = adapter_scale * total
    row[...] = grads
    squares = grads * grads
    down = factor_down[...]
    lane = lax.broadcasted_iota(jnp.int32, (1, 128), 1)
    line = jnp.where(
        lane < 64,
        jnp.where(lane < 32, jnp.sum(squares[:32]), jnp.sum(squares[32:88])),
        jnp.where(lane < 96, jnp.sum(down * down) * (1 / 8), total[88:89] + total[89:90]),
    )
    high = line.astype(bf16).astype(f32)
    low = line - high
    pair = lax.axis_index("zh")
    half = lax.axis_index("zl")
    for p in range(16):
        for odd in range(2):
            start = 32 + 7 * (4 * (p % 2) + pair) + (4 - half if odd else 0)
            columns_b = row[pl.ds(start, 4), :]
            for core in range(2):
                k = 4 * p + 2 * odd + core
                rows[k, 0:4] = row[4 * (p // 2) : 4 * (p // 2) + 4]
                rows[k, 4:8] = columns_b
                rows[k, 8:9] = high
                rows[k, 9:10] = low
                rows[k, 10:16] = jnp.zeros((6, 128), f32)
                out[k] = rows[k].astype(bf16)


def update_kernel(place, parts, factor_down, factor_up, base, new_down, new_up, merged, rows):
    line = jnp.zeros((1, 128), f32)
    for k in range(64):
        block = parts[k].astype(f32)
        rows[pl.ds(k * 17, 16), :] = block
        line += block[8:9] + block[9:10]
    scale_a = step_size * jnp.sqrt(line[:, 64:65]) / jnp.sqrt(line[:, 0:1] + norm_eps)
    scale_b = step_size * jnp.sqrt(line[:, 96:97]) / jnp.sqrt(line[:, 32:33] + norm_eps)

    def ranks(half, j):
        starts = [34 * half + 17 * core + 544 * h + j for core in range(2) for h in range(2)]
        return jnp.concatenate([rows[pl.ds(start, 8, 68), :] for start in starts], 0)

    for j in range(8):
        columns = slice(128 * j, 128 * j + 128)
        new_down[:, columns] = factor_down[:, columns] - scale_a * ranks(j // 4, j % 4)
    near, core = lax.axis_index("zl"), place[3]
    tiles = [ranks(near, 4 + 3 * core)]
    for j in range(1, 4):
        tiles.append(ranks(jnp.where(core == 0, near, 1 - near), 4 + j - core))
    grad_b = jnp.concatenate(tiles, 1)
    grad_b = jnp.where(core == 0, grad_b, pltpu.roll(grad_b, 448, 1))[:, :448]
    new_up[...] = factor_up[...] - scale_b * grad_b
    left = new_up[...].T.astype(bf16)
    right = new_down[...].astype(bf16)
    for k in range(7):
        lines = slice(64 * k, 64 * k + 64)
        product = jnp.dot(left[lines], right, preferred_element_type=f32)
        merged[lines] = (base[lines].astype(f32) + adapter_scale * product).astype(bf16)


def kernel(body, outs, args, scratch=(), in_hbm=(), mib=16, flops=0, moved=0):
    specs, placed = [], []
    for n, a in enumerate(args):
        if jnp.issubdtype(a.dtype, jnp.integer):
            specs.append(SMEM)
        else:
            specs.append(HBM if n in in_hbm else VMEM)
            a = pltpu.with_memory_space_constraint(a, pltpu.HBM if n in in_hbm else pltpu.VMEM)
        placed.append(a)
    return pl.pallas_call(
        body,
        out_shape=outs,
        in_specs=specs,
        out_specs=jax.tree.map(lambda _: VMEM, outs),
        scratch_shapes=list(scratch),
        compiler_params=pltpu.CompilerParams(vmem_limit_bytes=mib * 1024 * 1024),
        cost_estimate=pl.CostEstimate(flops=flops, bytes_accessed=moved, transcendentals=0),
        name=body.__name__,
    )(*placed)


def swap(x, axis):
    return lax.ppermute(x, axis, [(0, 1), (1, 0)])


def shards(tokens, grad_up, factor_down, factor_up, base_weight):
    place = jnp.stack([lax.axis_index(name) for name in ("xh", "y", "xl", "c")]).astype(jnp.int32)
    factor_up = factor_up.T
    shape = jax.ShapeDtypeStruct

    down, up = kernel(
        prepare_kernel,
        (shape((32, 1024), bf16), shape((16, 32, 512), bf16)),
        (factor_down, factor_up),
        [pltpu.VMEM((32, 1024), f32), pltpu.VMEM((32, 448), f32), pltpu.SemaphoreType.DMA((2,))],
        in_hbm=(0, 1),
    )
    down_far = swap(down, "xh")
    ups = exchange(up, ("xl", "zh", "zl"))
    down0 = jnp.stack([down, down_far])
    downs = [down0] + [lax.ppermute(down0, "y", [(i, i ^ k) for i in range(4)]) for k in (1, 2, 3)]
    ups, downs = lax.optimization_barrier((ups, downs))
    ups_other = swap(ups, "c")

    keep_b, give_b, tokens, grad_up = kernel(
        grad_b_kernel,
        [shape((16, 14336), bf16)] * 2 + [pltpu.VMEM((192, 8192), bf16), pltpu.VMEM((192, 14336), bf16)],
        [place, tokens, grad_up] + downs,
        [pltpu.VMEM((32, 8192), bf16), pltpu.SemaphoreType.DMA((16,))],
        in_hbm=(1, 2),
        flops=300000000,
        moved=10 * 1024 * 1024,
    )
    got_b = swap(give_b, "c")
    keep_a, give_a = kernel(
        grad_a_kernel,
        [shape((16, 8192), bf16)] * 2,
        (place, tokens, grad_up, ups, ups_other),
        [pltpu.VMEM((32, 14336), bf16)],
        flops=300000000,
        moved=10 * 1024 * 1024,
    )
    got_a = swap(give_a, "c")
    args = (keep_a, got_a, keep_b, got_b)
    parts = kernel(chip_sum_kernel, shape((32, 88, 128), bf16), args, [pltpu.VMEM((3008, 128), f32)])
    parts = exchange(parts, PLANE + ("zl",))
    parts = kernel(plane_sum_kernel, shape((4, 96, 128), bf16), (parts, factor_up), [pltpu.VMEM((96, 128), f32)])
    parts = exchange(parts, "zh")
    scratch = [pltpu.VMEM((96, 128), f32), pltpu.VMEM((64, 16, 128), f32)]
    parts = kernel(reroute_kernel, shape((64, 16, 128), bf16), (parts, factor_down), scratch)
    parts = exchange(parts, PLANE + ("zl", "c"))
    outs = (shape((32, 1024), f32), shape((32, 448), f32), shape((448, 1024), bf16))
    args = (place, parts, factor_down, factor_up, base_weight.T)
    new_down, new_up, merged = kernel(update_kernel, outs, args, [pltpu.VMEM((1160, 128), f32)])
    return (new_down, new_up.T, merged.T)


def solution(mesh):
    fine = Mesh(mesh.devices.reshape(2, 4, 2, 4, 2, 2), GRP + TP)
    return jax.shard_map(
        shards,
        mesh=fine,
        in_specs=(
            P(GRP + TP, None),
            P(GRP + TP, None),
            P(None, GRP),
            P(TP, None),
            P(GRP, TP),
        ),
        out_specs=(P(None, GRP), P(TP, None), P(GRP, TP)),
        check_vma=False,
    )
```
